256 devices in a mesh: ka: 16 (over x_lo, z), ga: 16 (over x_hi, y, core).
Axes of the slice: x: 4 (x_hi: 2, x_lo: 2; x = x_hi * 2 + x_lo), y: 4, z: 8, core: 2. Of those that a mesh axis runs over, the one named last changes fastest.
Arguments:
- initial_packet: float32 [32, 256, 64, 256], P('ka', 'ga'), may hold values from -6 to 6
- extents: int32 [32, 256], P('ka'), may hold values from 8 to 64, as said below
- potential: float32 [256, 64, 256], P('ga'), may hold values from 0 to 2
- coriolis_weight: float32 [256], P('ga'), may hold values from 0.005 to 0.03
- radial_kinetic: float32 [256, 256], replicated, as said below
- bond_kinetic: float32 [64, 64], replicated, as said below
- angle_kinetic: float32 [256, 256], replicated, as said below
Outputs:
- newest_packet: float32 [32, 256, 64, 256], P('ka', 'ga')
- former_packet: float32 [32, 256, 64, 256], P('ka', 'ga')
The draws below stay inside these ranges and needn't reach their ends.
Inputs may be any that keep to these rules, and one draw needn't show every extreme that they name: Grid points with bond index below extents[K, R] are live; extents[K, R] ≤ 64 − floor(3K/2) for every K and R, and some slab of block 0 is live over all 64 points. `radial_kinetic`: symmetric. `bond_kinetic`: symmetric. `angle_kinetic`: symmetric.
All inputs are finite; a program needn't handle non-finite values.
Results may differ from the reference program's by a relative error of at most 0.0001.
Values sent between devices are 32-bit elements; how exact they have to be, the bound alone decides.
No kernel may reach another device: no remote copies, remote signals or barrier semaphores. Data moves between devices by JAX's collectives and lax.ppermute only.
A program may use at most 128 MiB of HBM per device.

```python
import math
import jax
import jax.numpy as jnp
from jax import lax

NR = 256
NQ = 64
NA = 256
ITERS = 3
KBLK = 32
J = 31


def kinetic_matrix(key, order, spread):
    off_key, diag_key = jax.random.split(key)
    raw = jax.random.normal(off_key, (order, order), jnp.float32) * (spread / order ** 0.5)
    symmetric = (raw + raw.T) * 0.70710678
    diagonal = jax.random.uniform(diag_key, (order,), jnp.float32, 0.5, 1.5)
    return symmetric + jnp.eye(order, dtype=jnp.float32) * diagonal[None, :]


def draw_radial_kinetic(key, part):
    key = jax.random.fold_in(key, 11)
    return kinetic_matrix(key, NR, 0.5)


def draw_bond_kinetic(key, part):
    key = jax.random.fold_in(key, 12)
    return kinetic_matrix(key, NQ, 0.5)


def draw_angle_kinetic(key, part):
    key = jax.random.fold_in(key, 13)
    return kinetic_matrix(key, NA, 0.5)


def draw_extents(key, part):
    key = jax.random.fold_in(key, 7)
    pick_key, fill_key = jax.random.split(key)
    blocks = jnp.arange(KBLK, dtype=jnp.int32)[:, None]
    ceiling = NQ - NQ * 3 // 4 * blocks // KBLK
    values = jax.random.randint(fill_key, (KBLK, NR), NQ // 8, ceiling + 1, dtype=jnp.int32)
    picked = jax.random.randint(pick_key, (), 0, NR, dtype=jnp.int32)
    slabs = jnp.arange(NR, dtype=jnp.int32)[None, :]
    return jnp.where((blocks == 0) & (slabs == picked), NQ, values).astype(jnp.int32)


def level_of(own_key, dims, pieces, low, high):
    loudness, own = 1.0, jax.random.fold_in(own_key, 6)
    for dim, shards_of in pieces:
        heights = jnp.exp(jax.random.uniform(jax.random.fold_in(own, dim), (shards_of,), jnp.float32, low / len(pieces), high / len(pieces)))
        loudness = loudness * jnp.repeat(heights, dims[dim] // shards_of).reshape([-1 if axis == dim else 1 for axis in range(len(dims))])
    return loudness


def gaussian(own_key, shape, scale, bound, pieces=(), kind=jnp.bfloat16):
    gain = level_of(own_key, shape, pieces, -0.22, 0.18) if pieces else 1.0
    drawn = jax.random.normal(own_key, shape, jnp.float32) * scale * gain
    return jnp.minimum(jnp.maximum(drawn, -bound), bound).astype(kind)


def setup_inputs(seed: int = 0) -> dict:
    streams_of = jax.random.split(jax.random.key(seed), 8)
    initial_packet = gaussian(streams_of[0], (KBLK, NR, NQ, NA), 1.0, 6.0, ((0, 16), (1, 16)), jnp.float32)
    extents = draw_extents(jax.random.fold_in(streams_of[7], 71), 0)
    potential = jnp.clip(2.0 * jax.random.uniform(streams_of[2], (NR, NQ, NA), jnp.float32) ** level_of(streams_of[2], (NR, NQ, NA), ((0, 16),), -0.2, 0.2), 0.0, 2.0)
    coriolis_weight = jnp.clip(jnp.exp(math.log(0.03) - 1.7917595 * jax.random.uniform(streams_of[3], (NR,), jnp.float32) ** level_of(streams_of[3], (NR,), ((0, 16),), -0.2, 0.2)), 0.005, 0.03)
    radial_kinetic = draw_radial_kinetic(jax.random.fold_in(streams_of[7], 71), 0)
    bond_kinetic = draw_bond_kinetic(jax.random.fold_in(streams_of[7], 71), 0)
    angle_kinetic = draw_angle_kinetic(jax.random.fold_in(streams_of[7], 71), 0)
    return {"initial_packet": initial_packet, "extents": extents, "potential": potential, "coriolis_weight": coriolis_weight, "radial_kinetic": radial_kinetic, "bond_kinetic": bond_kinetic, "angle_kinetic": angle_kinetic}


energy_shift = 4.0
energy_spread = 7.0

def apply_scaled(packet, live_mask, potential, coriolis_weight, radial_kinetic, bond_kinetic, angle_kinetic, ladder_upper, ladder_lower):
    highest = lax.Precision.HIGHEST
    result = jnp.einsum('rs,ksqa->krqa', radial_kinetic, packet, precision=highest)
    result = result + jnp.einsum('qp,kspa->ksqa', bond_kinetic, packet, precision=highest)
    result = result + jnp.einsum('ab,ksqb->ksqa', angle_kinetic, packet, precision=highest)
    zeros_block = jnp.zeros_like(packet[:1])
    upper_block = jnp.concatenate([packet[1:], zeros_block], 0)
    lower_block = jnp.concatenate([zeros_block, packet[:-1]], 0)
    coupling = ladder_upper[:, None, None, None] * upper_block + ladder_lower[:, None, None, None] * lower_block
    result = result + potential[None] * packet - coriolis_weight[None, :, None, None] * coupling
    return live_mask * (result - energy_shift * packet) / energy_spread

def reference(initial_packet, extents, potential, coriolis_weight, radial_kinetic, bond_kinetic, angle_kinetic):
    bond_rows = jnp.arange(NQ, dtype=jnp.int32)
    live_mask = (bond_rows[None, None, :] < extents[:, :, None]).astype(jnp.float32)[..., None]
    kvalues = jnp.arange(KBLK, dtype=jnp.int32).astype(jnp.float32)
    total = jnp.float32(J * (J + 1))
    ladder_upper = jnp.sqrt(total - kvalues * (kvalues + 1.0))
    ladder_lower = jnp.sqrt(total - kvalues * (kvalues - 1.0))
    start = live_mask * initial_packet
    previous = start
    current = apply_scaled(start, live_mask, potential, coriolis_weight, radial_kinetic, bond_kinetic, angle_kinetic, ladder_upper, ladder_lower)
    for count in range(ITERS - 1):
        nextone = 2.0 * apply_scaled(current, live_mask, potential, coriolis_weight, radial_kinetic, bond_kinetic, angle_kinetic, ladder_upper, ladder_lower) - previous
        previous = current
        current = nextone
    return (current, previous)
```

```python
import functools

import jax
import jax.numpy as jnp
from jax import lax
from jax.experimental import pallas as pl
from jax.experimental.pallas import tpu as pltpu
from jax.sharding import PartitionSpec as P

SHIFT = 4.0
SPREAD = 7.0
CHIPS = 8
OCT = 8
F32 = jnp.float32
BF16 = jnp.bfloat16


def split(x):
    high = x.astype(BF16)
    return high, (x - high.astype(F32)).astype(BF16)


def mm(a, b):
    return jnp.dot(a, b, preferred_element_type=F32)


def params():
    return pltpu.CompilerParams(vmem_limit_bytes=32 * 1024 * 1024)


def prep(ids, radial, bond, angle):
    def kernel(ids, radial, bond, angle, rad_h, rad_l, bond_cat, ang_h, ang_l, tmp, tmpb):
        ga = ids[0]
        chip = ids[1]

        def rows(ref, count, size, own):
            return jnp.concatenate(
                [ref[pl.ds(pl.multiple_of((i ^ own) * size, size), size), :] for i in range(count)], 0
            )

        tmp[...] = rows(radial, 16, 16, ga).T
        high, low = split(rows(tmp, 16, 16, ga) / SPREAD)
        rad_h[...] = high
        rad_l[...] = low
        tmpb[...] = rows(bond, 8, 8, chip).T
        high, low = split(rows(tmpb, 8, 8, chip) / SPREAD)
        bond_cat[...] = jnp.concatenate([high, high, low], 1)
        high, low = split(angle[...].T / SPREAD)
        ang_h[...] = high
        ang_l[...] = low

    big = jax.ShapeDtypeStruct((256, 256), BF16)
    vm = pl.BlockSpec(memory_space=pltpu.VMEM)
    return pl.pallas_call(
        kernel,
        out_shape=(big, big, jax.ShapeDtypeStruct((64, 192), BF16), big, big),
        in_specs=[pl.BlockSpec(memory_space=pltpu.SMEM), vm, vm, vm],
        out_specs=(vm,) * 5,
        scratch_shapes=[pltpu.VMEM((256, 256), F32), pltpu.VMEM((128, 64), F32)],
        compiler_params=params(),
        name="prep",
    )(ids, radial, jnp.pad(bond, ((0, 64), (0, 64))), angle)


def start(ids, ext, own, other):
    def kernel(ids, ext, own, other, whole, *pieces):
        j = pl.program_id(0)
        row = (j ^ ids[1]) * OCT + lax.broadcasted_iota(jnp.int32, (OCT, 256), 0)
        for r in range(32):
            x = own[0, r] if r < 16 else other[r - 16]
            x = jnp.where(row < ext[r], x, 0.0)
            whole[0, r] = x
            for i in range(1, CHIPS):
                @pl.when(j == i)
                def _(i=i, r=r, x=x):
                    pieces[i - 1][r] = x

    piece = pl.BlockSpec((32, OCT, 256), lambda j, ids, ext: (0, 0, 0))
    return pl.pallas_call(
        kernel,
        grid_spec=pltpu.PrefetchScalarGridSpec(
            num_scalar_prefetch=2,
            grid=(CHIPS,),
            in_specs=[
                pl.BlockSpec((1, 16, OCT, 256), lambda j, ids, ext: (ids[2], 0, j ^ ids[1], 0)),
                pl.BlockSpec((16, OCT, 256), lambda j, ids, ext: (0, j ^ ids[1], 0)),
            ],
            out_specs=[pl.BlockSpec((1, 32, OCT, 256), lambda j, ids, ext: (j, 0, 0, 0))] + [piece] * 7,
        ),
        out_shape=[jax.ShapeDtypeStruct((CHIPS, 32, OCT, 256), F32)]
        + [jax.ShapeDtypeStruct((32, OCT, 256), F32)] * 7,
        compiler_params=params(),
        name="start",
    )(ids, ext, own, other)


def local_terms(ids, ext, coef, cur, near, far, pot, bond_cat, ang_h, ang_l, prev):
    step = 4

    def kernel(ids, ext, coef, cur, near, far, pot, bond_cat, ang_h, ang_l, *rest):
        prev, outs = (rest[0], rest[1:]) if len(rest) > CHIPS else (None, rest)
        first = pl.program_id(0) * step
        line = lax.broadcasted_iota(jnp.int32, (64, 256), 0)
        row = ((line >> 3) ^ ids[1]) * OCT + (line & 7)
        xs = [cur[:, r].reshape(64, 256) for r in range(step)]
        high, low = split(jnp.concatenate(xs, 0))
        angle = mm(high, ang_h[...]) + mm(low, ang_h[...]) + mm(high, ang_l[...])
        for r in range(step):
            part = slice(r * 64, r * 64 + 64)
            stack = jnp.concatenate([high[part], low[part], high[part]], 0)
            total = angle[part] + mm(bond_cat[...], stack)
            values = jnp.concatenate(
                [pot[r, pl.ds(pl.multiple_of((o ^ ids[1]) * OCT, OCT), OCT), :] for o in range(CHIPS)], 0
            )
            total = total + (values - SHIFT) * (1.0 / SPREAD) * xs[r]
            weight = coef[2 + first + r] * (1.0 / SPREAD)
            total = total - (weight * coef[0]) * near[:, r].reshape(64, 256)
            total = total - (weight * coef[1]) * far[:, r].reshape(64, 256)
            total = jnp.where(row < ext[first + r], total, 0.0)
            if prev is not None:
                total = 2.0 * total - prev[:, r].reshape(64, 256)
            for o in range(CHIPS):
                outs[o][r] = total[o * OCT : (o + 1) * OCT]

    whole = pl.BlockSpec((CHIPS, step, OCT, 256), lambda i: (0, i, 0, 0))
    crossed = pl.BlockSpec((CHIPS, step, OCT, 256), lambda i: (0, (i + 16 // step) % (32 // step), 0, 0))
    smem = pl.BlockSpec(memory_space=pltpu.SMEM)
    args = [ids, ext, coef, cur, near, far, pot, bond_cat, ang_h, ang_l]
    specs = [smem, smem, smem, whole, crossed, crossed, pl.BlockSpec((step, 64, 256), lambda i: (i, 0, 0))]
    specs += [
        pl.BlockSpec((64, 192), lambda i: (0, 0)),
        pl.BlockSpec((256, 256), lambda i: (0, 0)),
        pl.BlockSpec((256, 256), lambda i: (0, 0)),
    ]
    if prev is not None:
        args.append(prev)
        specs.append(whole)
    return pl.pallas_call(
        kernel,
        grid=(32 // step,),
        in_specs=specs,
        out_specs=[pl.BlockSpec((step, OCT, 256), lambda i: (i, 0, 0))] * CHIPS,
        out_shape=[jax.ShapeDtypeStruct((32, OCT, 256), F32)] * CHIPS,
        compiler_params=params(),
        cost_estimate=pl.CostEstimate(flops=2_000_000_000, bytes_accessed=14_000_000, transcendentals=0),
        name="local_terms",
    )(*args)


def radial_term(ids, ext_col, rad_h, rad_l, pieces, scale, more=None):
    flat = [p.reshape(256, 256) for p in pieces]
    if more is not None:
        flat += [p.reshape(256, 256) for p in more]
    count = len(flat)

    def kernel(ids, ext_col, rad_h, rad_l, *refs):
        ins, outs = refs[:count], refs[count:]

        def column(q):
            at = pl.ds(q, 32, stride=OCT)
            x = [ins[j][at, :] for j in range(CHIPS)]
            if count > CHIPS:
                x = [x[j] + ins[CHIPS + j][at, :] for j in range(CHIPS)]
            return jnp.concatenate(x, 0)

        for q in range(0, OCT, 2):
            high, low = split(jnp.concatenate([column(q), column(q + 1)], 1))
            total = mm(rad_h[...], high) + mm(rad_h[...], low) + mm(rad_l[...], high)
            for i in range(2):
                half = total[:, i * 128 : i * 128 + 128]
                half = jnp.where(ext_col[...] > ids[1] * OCT + q + i, half * scale, 0.0)
                for j in range(CHIPS):
                    outs[j][pl.ds(q + i, 32, stride=OCT), :] = half[j * 32 : j * 32 + 32]

    lanes = pl.BlockSpec((256, 128), lambda i: (0, i))
    full = pl.BlockSpec((256, 256), lambda i: (0, 0))
    out = pl.pallas_call(
        kernel,
        grid=(2,),
        in_specs=[
            pl.BlockSpec(memory_space=pltpu.SMEM), pl.BlockSpec((256, 1), lambda i: (0, 0)), full, full
        ] + [lanes] * count,
        out_specs=[lanes] * CHIPS,
        out_shape=[jax.ShapeDtypeStruct((256, 256), F32)] * CHIPS,
        compiler_params=params(),
        cost_estimate=pl.CostEstimate(flops=2_000_000_000, bytes_accessed=5_000_000, transcendentals=0),
        name="radial_term",
    )(ids, ext_col, rad_h, rad_l, *flat)
    return [o.reshape(32, OCT, 256) for o in out]


def finish(ids, own, other):
    def kernel(ids, own, other, out):
        out[ids[2]] = own[0]
        out[1 - ids[2]] = other[0]

    return pl.pallas_call(
        kernel,
        grid_spec=pltpu.PrefetchScalarGridSpec(
            num_scalar_prefetch=1,
            grid=(CHIPS,),
            in_specs=[
                pl.BlockSpec((1, 16, OCT, 256), lambda j, ids: (j, 0, 0, 0)),
                pl.BlockSpec((1, 16, OCT, 256), lambda j, ids: (j, 0, 0, 0)),
            ],
            out_specs=pl.BlockSpec((2, 16, OCT, 256), lambda j, ids: (0, 0, j ^ ids[1], 0)),
        ),
        out_shape=jax.ShapeDtypeStruct((2, 16, 64, 256), F32),
        compiler_params=params(),
        name="finish",
    )(ids, own, other)


def shards(initial_packet, extents, potential, coriolis_weight, radial_kinetic, bond_kinetic, angle_kinetic):
    ka, ga = lax.axis_index("ka"), lax.axis_index("ga")
    chip, core = ga // 2, ga % 2
    ids = jnp.stack([ga, chip, core]).astype(jnp.int32)
    groups = lax.axis_size("ka")
    members = lax.axis_size("ga")
    top = jnp.float32((2 * groups - 1) * (2 * groups))

    def swap_core(x):
        return lax.ppermute(x, "ga", [(g, g ^ 1) for g in range(members)])

    def swap_chip(x, j):
        return lax.ppermute(x, "ga", [(g, g ^ (2 * j)) for g in range(members)])

    far_pairs = []
    for i in range(groups):
        for g in range(members):
            target = i + 1 if g % 2 else i - 1
            if 0 <= target < groups:
                far_pairs.append((i * members + g, target * members + (g ^ 1)))

    def halo(x):
        return swap_core(x), lax.ppermute(x, ("ka", "ga"), far_pairs)

    def exchange(pieces):
        return [pieces[0]] + [swap_chip(pieces[j], j) for j in range(1, CHIPS)]

    other = swap_core(lax.dynamic_index_in_dim(initial_packet, 1 - core, 0, keepdims=False))
    pot = jnp.concatenate([potential, swap_core(potential)], 0)
    weight = jnp.concatenate([coriolis_weight, swap_core(coriolis_weight)])
    kvalue = (2 * ka + core).astype(F32)
    upper = jnp.sqrt(top - kvalue * (kvalue + 1.0))
    lower = jnp.sqrt(top - kvalue * (kvalue - 1.0))
    coef = jnp.concatenate(
        [jnp.stack([jnp.where(core == 0, upper, lower), jnp.where(core == 0, lower, upper)]), weight]
    )
    ext = lax.dynamic_index_in_dim(extents, core, 0, keepdims=False).reshape(16, 16)
    ext = ext[jnp.arange(16) ^ ga].reshape(256)
    ext_col = ext[:, None]
    ext = ext[:32]

    rad_h, rad_l, bond_cat, ang_h, ang_l = prep(ids, radial_kinetic, bond_kinetic, angle_kinetic)

    def local(cur, halos, prev=None):
        return local_terms(ids, ext, coef, cur, *halos, pot, bond_cat, ang_h, ang_l, prev)

    def radial(pieces, scale, more=None):
        return radial_term(ids, ext_col, rad_h, rad_l, pieces, scale, more)

    def add(a, b):
        return [x + y for x, y in zip(a, b)]

    def outputs(whole):
        return finish(ids, whole, swap_core(whole[:, 16:]))

    t0, *p0 = start(ids, ext, initial_packet, other)
    p0 = [t0[0]] + p0
    p0_far = exchange(p0)
    a0 = local(t0, halo(t0))
    b0 = radial(p0_far, 1.0)
    a0_far = exchange(a0)
    t1 = jnp.stack(add(a0, exchange(b0)))
    b1 = radial(a0_far, 2.0, b0)
    c1 = local(t1, halo(t1), t0)
    p2 = add(c1, exchange(b1))
    t2 = jnp.stack(p2)
    p2_far = exchange(p2)
    c2 = local(t2, halo(t2), t1)
    b2 = radial(p2_far, 2.0)
    t3 = jnp.stack(add(c2, exchange(b2)))
    return outputs(t3), outputs(t2)


def solution(mesh):
    return jax.shard_map(
        shards,
        mesh=mesh,
        in_specs=(
            P("ka", "ga", None, None),
            P("ka", None),
            P("ga", None, None),
            P("ga"),
            P(),
            P(),
            P(),
        ),
        out_specs=(P("ka", "ga", None, None), P("ka", "ga", None, None)),
        check_vma=False,
    )
```

```python
import functools

import jax
import jax.numpy as jnp
from jax import lax
from jax.experimental import pallas as pl
from jax.experimental.pallas import tpu as pltpu
from jax.sharding import PartitionSpec as P

SHIFT = 4.0
SPREAD = 7.0
CHIPS = 8
OCT = 8
CUTS = (3, 5)
F32 = jnp.float32
BF16 = jnp.bfloat16


def split(x):
    high = x.astype(BF16)
    return high, (x - high.astype(F32)).astype(BF16)


def mm(a, b):
    return jnp.dot(a, b, preferred_element_type=F32)


def params():
    return pltpu.CompilerParams(vmem_limit_bytes=32 * 1024 * 1024)


def prep(ids, radial, bond, angle):
    def kernel(ids, radial, bond, angle, rad_h, rad_l, bond_cat, ang_h, ang_l, tmp):
        def rows(ref):
            return jnp.concatenate(
                [ref[pl.ds(pl.multiple_of((i ^ ids[1]) * 16, 16), 16), :] for i in range(16)], 0
            )

        tmp[...] = rows(radial).T
        rad_h[...], rad_l[...] = split(rows(tmp) / SPREAD)
        high, low = split(bond[...] / SPREAD)
        bond_cat[...] = jnp.concatenate([high, high, low], 1)
        ang_h[...], ang_l[...] = split(angle[...].T / SPREAD)

    big = jax.ShapeDtypeStruct((256, 256), BF16)
    vm = pl.BlockSpec(memory_space=pltpu.VMEM)
    return pl.pallas_call(
        kernel,
        out_shape=(big, big, jax.ShapeDtypeStruct((64, 192), BF16), big, big),
        in_specs=[pl.BlockSpec(memory_space=pltpu.SMEM), vm, vm, vm],
        out_specs=(vm,) * 5,
        scratch_shapes=[pltpu.VMEM((256, 256), F32)],
        compiler_params=params(),
        name="prep",
    )(ids, radial, bond, angle)


def start(ids, ext, own, other):
    step = 8
    half = 16 // step

    def kernel(ids, ext, own, other, whole):
        i = pl.program_id(0)
        line = lax.broadcasted_iota(jnp.int32, (64, 256), 0)
        for r in range(step):
            x = jnp.where(i < half, own[0, r], other[r])
            whole[:, r] = jnp.where(line < ext[i * step + r], x, 0.0).reshape(CHIPS, OCT, 256)

    return pl.pallas_call(
        kernel,
        grid_spec=pltpu.PrefetchScalarGridSpec(
            num_scalar_prefetch=2,
            grid=(32 // step,),
            in_specs=[
                pl.BlockSpec((1, step, 64, 256), lambda i, ids, ext: (ids[1], jnp.minimum(i, half - 1), 0, 0)),
                pl.BlockSpec((step, 64, 256), lambda i, ids, ext: (jnp.maximum(i - half, 0), 0, 0)),
            ],
            out_specs=pl.BlockSpec((CHIPS, step, OCT, 256), lambda i, ids, ext: (0, i, 0, 0)),
        ),
        out_shape=pltpu.HBM((CHIPS, 32, OCT, 256), F32),
        compiler_params=params(),
        name="start",
    )(ids, ext, own, other)


def local_terms(ext, coef, cur, near, far, far_mid, far_top, pot, bond_cat, ang_h, ang_l, prev):
    step = 4

    def kernel(ext, coef, cur, near, far, far_mid, far_top, pot, bond_cat, ang_h, ang_l, *rest):
        prev, out = (rest[0], rest[1]) if len(rest) > 1 else (None, rest[0])
        first = pl.program_id(0) * step
        line = lax.broadcasted_iota(jnp.int32, (64, 256), 0)
        xs = [cur[:, r].reshape(64, 256) for r in range(step)]
        high, low = split(jnp.concatenate(xs, 0))
        angle = mm(high, ang_h[...]) + mm(low, ang_h[...]) + mm(high, ang_l[...])
        for r in range(step):
            part = slice(r * 64, r * 64 + 64)
            stack = jnp.concatenate([high[part], low[part], high[part]], 0)
            total = angle[part] + mm(bond_cat[...], stack)
            total = total + (pot[r] - SHIFT) * (1.0 / SPREAD) * xs[r]
            weight = coef[2 + first + r] * (1.0 / SPREAD)
            total = total - (weight * coef[0]) * near[:, r].reshape(64, 256)
            total = total - (weight * coef[1]) * jnp.concatenate(
                [f[:, r].reshape(-1, 256) for f in (far, far_mid, far_top)], 0
            )
            total = jnp.where(line < ext[first + r], total, 0.0)
            if prev is not None:
                total = 2.0 * total - prev[:, r].reshape(64, 256)
            out[:, r] = total.reshape(CHIPS, OCT, 256)

    whole = pl.BlockSpec((CHIPS, step, OCT, 256), lambda i: (0, i, 0, 0))
    def crossed(count):
        return pl.BlockSpec((count, step, OCT, 256), lambda i: (0, (i + 16 // step) % (32 // step), 0, 0))

    smem = pl.BlockSpec(memory_space=pltpu.SMEM)
    args = [ext, coef, cur, near, far, far_mid, far_top, pot, bond_cat, ang_h, ang_l]
    specs = [smem, smem, whole, crossed(CHIPS), crossed(CUTS[0]), crossed(CUTS[1] - CUTS[0]), crossed(CHIPS - CUTS[1]), pl.BlockSpec((step, 64, 256), lambda i: (i, 0, 0))]
    specs += [
        pl.BlockSpec((64, 192), lambda i: (0, 0)),
        pl.BlockSpec((256, 256), lambda i: (0, 0)),
        pl.BlockSpec((256, 256), lambda i: (0, 0)),
    ]
    if prev is not None:
        args.append(prev)
        specs.append(whole)
    return pl.pallas_call(
        kernel,
        grid=(32 // step,),
        in_specs=specs,
        out_specs=whole,
        out_shape=pltpu.HBM((CHIPS, 32, OCT, 256), F32),
        compiler_params=params(),
        cost_estimate=pl.CostEstimate(flops=2_000_000_000, bytes_accessed=14_000_000, transcendentals=0),
        name="local_terms",
    )(*args)


def radial_term(ids, ext_col, rad_h, rad_l, packet, scale, more=None):
    rows = CHIPS * 32 * OCT
    flat = [p.reshape(rows, 256) for p in ((packet,) if more is None else (packet, more))]
    count = len(flat)

    def kernel(ids, ext_col, rad_h, rad_l, *refs):
        ins, out = refs[:count], refs[count]

        def column(q):
            at = pl.ds(q, 256, stride=OCT)
            return ins[0][at, :] + ins[1][at, :] if count > 1 else ins[0][at, :]

        for q in range(0, OCT, 2):
            high, low = split(jnp.concatenate([column(q), column(q + 1)], 1))
            total = mm(rad_h[...], high) + mm(rad_h[...], low) + mm(rad_l[...], high)
            for i in range(2):
                half = total[:, i * 128 : i * 128 + 128]
                half = jnp.where(ext_col[...] > ids[0] * OCT + q + i, half * scale, 0.0)
                out[pl.ds(q + i, 256, stride=OCT), :] = half

    lanes = pl.BlockSpec((rows, 128), lambda i: (0, i))
    full = pl.BlockSpec((256, 256), lambda i: (0, 0))
    out = pl.pallas_call(
        kernel,
        grid=(2,),
        in_specs=[
            pl.BlockSpec(memory_space=pltpu.SMEM), pl.BlockSpec((256, 1), lambda i: (0, 0)), full, full
        ] + [lanes] * count,
        out_specs=lanes,
        out_shape=pltpu.HBM((rows, 256), F32),
        compiler_params=params(),
        cost_estimate=pl.CostEstimate(flops=2_000_000_000, bytes_accessed=5_000_000, transcendentals=0),
        name="radial_term",
    )(ids, ext_col, rad_h, rad_l, *flat)
    return out.reshape(CHIPS, 32, OCT, 256)


def finish(ids, own, other):
    def kernel(ids, own, other, out):
        out[ids[1]] = own[0]
        out[1 - ids[1]] = other[0]

    return pl.pallas_call(
        kernel,
        grid_spec=pltpu.PrefetchScalarGridSpec(
            num_scalar_prefetch=1,
            grid=(CHIPS,),
            in_specs=[
                pl.BlockSpec((1, 16, OCT, 256), lambda j, ids: (j, 0, 0, 0)),
                pl.BlockSpec((1, 16, OCT, 256), lambda j, ids: (j, 0, 0, 0)),
            ],
            out_specs=pl.BlockSpec((2, 16, OCT, 256), lambda j, ids: (0, 0, j, 0)),
        ),
        out_shape=jax.ShapeDtypeStruct((2, 16, 64, 256), F32),
        compiler_params=params(),
        name="finish",
    )(ids, own, other)


def shards(initial_packet, extents, potential, coriolis_weight, radial_kinetic, bond_kinetic, angle_kinetic):
    ka, ga = lax.axis_index("ka"), lax.axis_index("ga")
    chip, core = ga // 2, ga % 2
    ids = jnp.stack([chip, core]).astype(jnp.int32)
    groups = lax.axis_size("ka")
    members = lax.axis_size("ga")
    top = jnp.float32((2 * groups - 1) * (2 * groups))

    def swap_core(x):
        return lax.ppermute(x, "ga", [(g, g ^ 1) for g in range(members)])

    def swap_far(x, octets):
        count = groups if octets.start < CUTS[1] else groups // 2
        pairs = [
            (i * members + g, k * members + (g ^ 1))
            for i in range(count)
            for g in range(members)
            for k in (i + 1 if g % 2 else i - 1,)
            if 0 <= k < count
        ]
        return lax.ppermute(x[octets], ("ka", "ga"), pairs)

    def halo(t, turned):
        near = swap_core(t)
        low = swap_far(t, slice(0, CUTS[0]))
        top = swap_far(t, slice(CUTS[1], CHIPS))
        turned, near, low, top = lax.optimization_barrier((turned, near, low, top))
        t, turned = lax.optimization_barrier((t, turned))
        return turned, (near, low, swap_far(t, slice(*CUTS)), top)

    same_core = [list(range(c, members, 2)) for c in range(2)]

    def turn(x):
        return lax.all_to_all(x, "ga", 0, 0, axis_index_groups=same_core, tiled=True)

    other = swap_core(lax.dynamic_index_in_dim(initial_packet, 1 - core, 0, keepdims=False))
    pot = jnp.concatenate([potential, swap_core(potential)], 0)
    weight = jnp.concatenate([coriolis_weight, swap_core(coriolis_weight)])
    kvalue = (2 * ka + core).astype(F32)
    upper = jnp.sqrt(top - kvalue * (kvalue + 1.0))
    lower = jnp.where(kvalue > 0.0, jnp.sqrt(top - kvalue * (kvalue - 1.0)), 0.0)
    coef = jnp.concatenate(
        [jnp.stack([jnp.where(core == 0, upper, lower), jnp.where(core == 0, lower, upper)]), weight]
    )
    ext = lax.dynamic_index_in_dim(extents, core, 0, keepdims=False).reshape(16, 16)
    ext = jnp.where(core == 0, ext, ext.reshape(8, 2, 16)[:, ::-1].reshape(16, 16)).reshape(256)
    ext_col = ext[:, None]
    ext = lax.dynamic_slice_in_dim(ext, chip * 32, 32)

    rad_h, rad_l, bond_cat, ang_h, ang_l = prep(ids, radial_kinetic, bond_kinetic, angle_kinetic)

    def local(cur, halos, prev=None):
        return local_terms(ext, coef, cur, *halos, pot, bond_cat, ang_h, ang_l, prev)

    def radial(packet, scale, more=None):
        return radial_term(ids, ext_col, rad_h, rad_l, packet, scale, more)

    def outputs(whole):
        return finish(ids, whole, swap_core(whole[:, 16:]))

    t0 = start(ids, ext, initial_packet, other)
    turned, h0 = halo(t0, turn(t0))
    b0 = radial(turned, 1.0)
    a0 = local(t0, h0)
    t1 = a0 + turn(b0)
    turned, h1 = halo(t1, turn(a0))
    b1 = radial(turned, 2.0, b0)
    c1 = local(t1, h1, t0)
    t2 = c1 + turn(b1)
    turned, h2 = halo(t2, turn(t2))
    b2 = radial(turned, 2.0)
    c2 = local(t2, h2, t1)
    former = outputs(t2)
    c2, former = lax.optimization_barrier((c2, former))
    t3 = c2 + turn(b2)
    return outputs(t3), former


def solution(mesh):
    return jax.shard_map(
        shards,
        mesh=mesh,
        in_specs=(
            P("ka", "ga", None, None),
            P("ka", None),
            P("ga", None, None),
            P("ga"),
            P(),
            P(),
            P(),
        ),
        out_specs=(P("ka", "ga", None, None), P("ka", "ga", None, None)),
        check_vma=False,
    )
```

```python
import functools

import jax
import jax.numpy as jnp
from jax import lax
from jax.experimental import pallas as pl
from jax.experimental.pallas import tpu as pltpu
from jax.sharding import PartitionSpec as P

SHIFT = 4.0
SPREAD = 7.0
CHIPS = 8
OCT = 8
BOUNDS = ((0, 3), (3, 5), (5, 8))
F32 = jnp.float32
BF16 = jnp.bfloat16


def split(x):
    high = x.astype(BF16)
    return high, (x - high.astype(F32)).astype(BF16)


def mm(a, b):
    return jnp.dot(a, b, preferred_element_type=F32)


def params(mib=24):
    return pltpu.CompilerParams(vmem_limit_bytes=mib * 1024 * 1024)


def extent(ids, ext, r):
    return ext[ids[1], ids[0] * 32 + ((r // 16) ^ ids[1]) * 16 + r % 16]


def prep(ids, radial, bond, angle, extents):
    def kernel(ids, radial, bond, angle, extents, rad, bond_cat, ang, ext_col, tmp, tmp_col):
        def rows(ref):
            return jnp.concatenate(
                [ref[pl.ds(pl.multiple_of((i ^ ids[1]) * 16, 16), 16), :] for i in range(16)], 0
            )

        tmp[...] = rows(radial).T
        rad[0], rad[1] = split(rows(tmp) / SPREAD)
        high, low = split(bond[...] / SPREAD)
        bond_cat[...] = jnp.concatenate([high, high, low], 1)
        ang[0], ang[1] = split(angle[...].T / SPREAD)
        line = jnp.where(ids[1] == 0, extents[0:1], extents[1:2]).astype(F32)
        tmp_col[...] = jnp.broadcast_to(line, (128, 256)).T
        ext_col[...] = rows(tmp_col)

    big = jax.ShapeDtypeStruct((2, 256, 256), BF16)
    vm = pl.BlockSpec(memory_space=pltpu.VMEM)
    return pl.pallas_call(
        kernel,
        out_shape=(big, jax.ShapeDtypeStruct((64, 192), BF16), big, jax.ShapeDtypeStruct((256, 128), F32)),
        in_specs=[pl.BlockSpec(memory_space=pltpu.SMEM), vm, vm, vm, vm],
        out_specs=(vm,) * 4,
        scratch_shapes=[pltpu.VMEM((256, 256), F32), pltpu.VMEM((256, 128), F32)],
        compiler_params=params(),
        name="prep",
    )(ids, radial, bond, angle, extents)


def start(ids, ext, own, other):
    step = 8
    half = 16 // step

    def kernel(ids, ext, own, other, whole):
        i = pl.program_id(0)
        line = lax.broadcasted_iota(jnp.int32, (64, 256), 0)
        for r in range(step):
            x = jnp.where(i < half, own[0, r], other[r])
            whole[:, r] = jnp.where(line < extent(ids, ext, i * step + r), x, 0.0).reshape(CHIPS, OCT, 256)

    return pl.pallas_call(
        kernel,
        grid_spec=pltpu.PrefetchScalarGridSpec(
            num_scalar_prefetch=2,
            grid=(32 // step,),
            in_specs=[
                pl.BlockSpec((1, step, 64, 256), lambda i, ids, ext: (ids[1], jnp.minimum(i, half - 1), 0, 0)),
                pl.BlockSpec((step, 64, 256), lambda i, ids, ext: (jnp.maximum(i - half, 0), 0, 0)),
            ],
            out_specs=pl.BlockSpec((CHIPS, step, OCT, 256), lambda i, ids, ext: (0, i, 0, 0)),
        ),
        out_shape=pltpu.HBM((CHIPS, 32, OCT, 256), F32),
        compiler_params=params(),
        name="start",
    )(ids, ext, own, other)


def local_terms(ids, ext, coef, cur, near, far, far_mid, far_top, pot, bond_cat, ang, prev, sent):
    step = 4

    def kernel(ids, ext, coef, cur, near, far, far_mid, far_top, pot, bond_cat, ang, *rest):
        prev, out = (rest[0], rest[1]) if len(rest) > 1 else (None, rest[0])
        first = pl.program_id(0) * step
        line = lax.broadcasted_iota(jnp.int32, (64, 256), 0)
        xs = [cur[:, r].reshape(64, 256) for r in range(step)]
        high, low = split(jnp.concatenate(xs, 0))
        angle = mm(high, ang[0]) + mm(low, ang[0]) + mm(high, ang[1])
        for r in range(step):
            part = slice(r * 64, r * 64 + 64)
            stack = jnp.concatenate([high[part], low[part], high[part]], 0)
            total = angle[part] + mm(bond_cat[...], stack)
            total = total + (pot[r] - SHIFT) * (1.0 / SPREAD) * xs[r]
            weight = coef[2 + first + r] * (1.0 / SPREAD)
            total = total - (weight * coef[0]) * near[:, r].reshape(64, 256)
            total = total - (weight * coef[1]) * jnp.concatenate(
                [f[:, r].reshape(-1, 256) for f in (far, far_mid, far_top)], 0
            )
            total = jnp.where(line < extent(ids, ext, first + r), total, 0.0)
            if prev is not None:
                total = 2.0 * total - prev[:, r].reshape(64, 256)
            out[:, r] = total.reshape(CHIPS, OCT, 256)

    whole = pl.BlockSpec((CHIPS, step, OCT, 256), lambda i: (0, i, 0, 0))
    def crossed(count):
        return pl.BlockSpec((count, step, OCT, 256), lambda i: (0, (i + 16 // step) % (32 // step), 0, 0))

    smem = pl.BlockSpec(memory_space=pltpu.SMEM)
    args = [ids, ext, coef, cur, near, far, far_mid, far_top, pot, bond_cat, ang]
    specs = [smem, smem, smem, whole, crossed(CHIPS), *[crossed(hi - lo) for lo, hi in BOUNDS], pl.BlockSpec((step, 64, 256), lambda i: (i, 0, 0))]
    specs += [
        pl.BlockSpec((64, 192), lambda i: (0, 0)),
        pl.BlockSpec((2, 256, 256), lambda i: (0, 0, 0)),
    ]
    if prev is not None:
        args.append(prev)
        specs.append(whole)
    return pl.pallas_call(
        kernel,
        grid=(32 // step,),
        in_specs=specs,
        out_specs=whole,
        out_shape=(pltpu.HBM if sent else jax.ShapeDtypeStruct)((CHIPS, 32, OCT, 256), F32),
        compiler_params=params(),
        cost_estimate=pl.CostEstimate(flops=2_000_000_000, bytes_accessed=14_000_000, transcendentals=0),
        name="local_terms",
    )(*args)


def radial_term(ids, ext_col, rad, packet, scale, more=None):
    rows = CHIPS * 32 * OCT
    flat = [p.reshape(rows, 256) for p in ((packet,) if more is None else (packet, more))]
    count = len(flat)

    def kernel(ids, ext_col, rad, *refs):
        ins, out = refs[:count], refs[count]

        def column(q):
            at = pl.ds(q, 256, stride=OCT)
            return ins[0][at, :] + ins[1][at, :] if count > 1 else ins[0][at, :]

        for q in range(0, OCT, 2):
            high, low = split(jnp.concatenate([column(q), column(q + 1)], 1))
            total = mm(rad[0], high) + mm(rad[0], low) + mm(rad[1], high)
            for i in range(2):
                half = total[:, i * 128 : i * 128 + 128]
                half = jnp.where(ext_col[...] > (ids[0] * OCT + q + i).astype(F32), half * scale, 0.0)
                out[pl.ds(q + i, 256, stride=OCT), :] = half

    lanes = pl.BlockSpec((rows, 128), lambda i: (0, i))
    full = pl.BlockSpec((2, 256, 256), lambda i: (0, 0, 0))
    out = pl.pallas_call(
        kernel,
        grid=(2,),
        in_specs=[
            pl.BlockSpec(memory_space=pltpu.SMEM), pl.BlockSpec((256, 128), lambda i: (0, 0)), full
        ] + [lanes] * count,
        out_specs=lanes,
        out_shape=pltpu.HBM((rows, 256), F32),
        compiler_params=params(56),
        cost_estimate=pl.CostEstimate(flops=2_000_000_000, bytes_accessed=5_000_000, transcendentals=0),
        name="radial_term",
    )(ids, ext_col, rad, *flat)
    return out.reshape(CHIPS, 32, OCT, 256)


def finish(ids, own, other, more=None):
    step = 2
    ins = (own, other) if more is None else (own, other, more)

    def kernel(ids, own, other, *rest):
        out = rest[-1]
        for o in range(step):
            at = slice(o * OCT, o * OCT + OCT)
            out[ids[1], :, at, :] = own[o] + rest[0][o] if len(rest) > 1 else own[o]
            out[1 - ids[1], :, at, :] = other[o]

    return pl.pallas_call(
        kernel,
        grid_spec=pltpu.PrefetchScalarGridSpec(
            num_scalar_prefetch=1,
            grid=(CHIPS // step,),
            in_specs=[pl.BlockSpec((step, 16, OCT, 256), lambda j, ids: (j, 0, 0, 0))] * len(ins),
            out_specs=pl.BlockSpec((2, 16, step * OCT, 256), lambda j, ids: (0, 0, j, 0)),
        ),
        out_shape=jax.ShapeDtypeStruct((2, 16, 64, 256), F32),
        compiler_params=params(),
        name="finish",
    )(ids, *ins)


def shards(initial_packet, extents, potential, coriolis_weight, radial_kinetic, bond_kinetic, angle_kinetic):
    ka, ga = lax.axis_index("ka"), lax.axis_index("ga")
    chip, core = ga // 2, ga % 2
    ids = jnp.stack([chip, core]).astype(jnp.int32)
    groups = lax.axis_size("ka")
    members = lax.axis_size("ga")
    top = jnp.float32((2 * groups - 1) * (2 * groups))

    def swap_core(x):
        return lax.ppermute(x, "ga", [(g, g ^ 1) for g in range(members)])

    def swap_far(x, count):
        pairs = [
            (i * members + g, k * members + (g ^ 1))
            for i in range(count)
            for g in range(members)
            for k in (i + 1 if g % 2 else i - 1,)
            if 0 <= k < count
        ]
        return lax.ppermute(x, ("ka", "ga"), pairs)

    def halo(t, turned):
        low, mid, top = [t[lo:hi] for lo, hi in BOUNDS]
        low, top = swap_far(low, groups), swap_far(top, groups // 2)
        turned, low, top = lax.optimization_barrier((turned, low, top))
        t, mid, turned = lax.optimization_barrier((t, mid, turned))
        return turned, (swap_core(t), low, swap_far(mid, groups), top)

    same_core = [list(range(c, members, 2)) for c in range(2)]

    def turn(x):
        return lax.all_to_all(x, "ga", 0, 0, axis_index_groups=same_core, tiled=True)

    other = swap_core(lax.dynamic_index_in_dim(initial_packet, 1 - core, 0, keepdims=False))
    pot = jnp.concatenate([potential, swap_core(potential)], 0)
    weight = jnp.concatenate([coriolis_weight, swap_core(coriolis_weight)])
    kvalue = (2 * ka + core).astype(F32)
    upper = jnp.sqrt(top - kvalue * (kvalue + 1.0))
    lower = jnp.where(kvalue > 0.0, jnp.sqrt(top - kvalue * (kvalue - 1.0)), 0.0)
    coef = jnp.concatenate(
        [jnp.stack([jnp.where(core == 0, upper, lower), jnp.where(core == 0, lower, upper)]), weight]
    )
    rad, bond_cat, ang, ext_col = prep(ids, radial_kinetic, bond_kinetic, angle_kinetic, extents)
    other, rad, bond_cat, ang, ext_col = lax.optimization_barrier((other, rad, bond_cat, ang, ext_col))

    def local(cur, halos, prev=None, sent=True):
        return local_terms(ids, extents, coef, cur, *halos, pot, bond_cat, ang, prev, sent)

    def radial(packet, scale, more=None):
        return radial_term(ids, ext_col, rad, packet, scale, more)

    t0 = start(ids, extents, initial_packet, other)
    turned, h0 = halo(t0, turn(t0))
    b0 = radial(turned, 1.0)
    a0 = local(t0, h0)
    t1 = a0 + turn(b0)
    turned, h1 = halo(t1, turn(a0))
    b1 = radial(turned, 2.0, b0)
    c1 = local(t1, h1, t0)
    t2 = c1 + turn(b1)
    turned, h2 = halo(t2, turn(c1))
    b2 = radial(turned, 2.0, b1)
    c2 = local(t2, h2, t1, sent=False)
    former = finish(ids, t2, swap_core(t2[:, 16:]))
    c2, former = lax.optimization_barrier((c2, former))
    b2 = turn(b2)
    newest = finish(ids, c2, swap_core(c2[:, 16:] + b2[:, 16:]), b2)
    return newest, former


def solution(mesh):
    return jax.shard_map(
        shards,
        mesh=mesh,
        in_specs=(
            P("ka", "ga", None, None),
            P("ka", None),
            P("ga", None, None),
            P("ga"),
            P(),
            P(),
            P(),
        ),
        out_specs=(P("ka", "ga", None, None), P("ka", "ga", None, None)),
        check_vma=False,
    )
```

```python
import functools

import jax
import jax.numpy as jnp
from jax import lax
from jax.experimental import pallas as pl
from jax.experimental.pallas import tpu as pltpu
from jax.sharding import PartitionSpec as P

SHIFT = 4.0
SPREAD = 7.0
CHIPS = 8
OCT = 8
BOUNDS = ((0, 2), (2, 5), (5, 8))
F32 = jnp.float32
BF16 = jnp.bfloat16


def split(x):
    high = x.astype(BF16)
    return high, (x - high.astype(F32)).astype(BF16)


def mm(a, b):
    return jnp.dot(a, b, preferred_element_type=F32)


def params(mib=24):
    return pltpu.CompilerParams(vmem_limit_bytes=mib * 1024 * 1024)


def extent(ids, ext, r):
    return ext[ids[1], ids[0] * 32 + ((r // 16) ^ ids[1]) * 16 + r % 16]


def prep(ids, radial, bond, angle, extents):
    def kernel(ids, radial, bond, angle, extents, rad, bond_cat, ang, ext_col, tmp, tmp_col):
        def rows(ref):
            return jnp.concatenate(
                [ref[pl.ds(pl.multiple_of((i ^ ids[1]) * 16, 16), 16), :] for i in range(16)], 0
            )

        tmp[...] = rows(radial).T
        rad[0], rad[1] = split(rows(tmp) / SPREAD)
        high, low = split(bond[...] / SPREAD)
        bond_cat[...] = jnp.concatenate([high, high, low], 1)
        ang[0], ang[1] = split(angle[...].T / SPREAD)
        line = jnp.where(ids[1] == 0, extents[0:1], extents[1:2]).astype(F32)
        tmp_col[...] = jnp.broadcast_to(line, (128, 256)).T
        ext_col[...] = rows(tmp_col)

    big = jax.ShapeDtypeStruct((2, 256, 256), BF16)
    vm = pl.BlockSpec(memory_space=pltpu.VMEM)
    return pl.pallas_call(
        kernel,
        out_shape=(big, jax.ShapeDtypeStruct((64, 192), BF16), big, jax.ShapeDtypeStruct((256, 128), F32)),
        in_specs=[pl.BlockSpec(memory_space=pltpu.SMEM), vm, vm, vm, vm],
        out_specs=(vm,) * 4,
        scratch_shapes=[pltpu.VMEM((256, 256), F32), pltpu.VMEM((256, 128), F32)],
        compiler_params=params(),
        name="prep",
    )(ids, radial, bond, angle, extents)


def start(ids, ext, own, other):
    step = 8
    half = 16 // step

    def kernel(ids, ext, own, other, whole):
        i = pl.program_id(0)
        line = lax.broadcasted_iota(jnp.int32, (64, 256), 0)
        for r in range(step):
            x = jnp.where(i < half, own[0, r], other[r])
            whole[:, r] = jnp.where(line < extent(ids, ext, i * step + r), x, 0.0).reshape(CHIPS, OCT, 256)

    return pl.pallas_call(
        kernel,
        grid_spec=pltpu.PrefetchScalarGridSpec(
            num_scalar_prefetch=2,
            grid=(32 // step,),
            in_specs=[
                pl.BlockSpec((1, step, 64, 256), lambda i, ids, ext: (ids[1], jnp.minimum(i, half - 1), 0, 0)),
                pl.BlockSpec((step, 64, 256), lambda i, ids, ext: (jnp.maximum(i - half, 0), 0, 0)),
            ],
            out_specs=pl.BlockSpec((CHIPS, step, OCT, 256), lambda i, ids, ext: (0, i, 0, 0)),
        ),
        out_shape=pltpu.HBM((CHIPS, 32, OCT, 256), F32),
        compiler_params=params(),
        name="start",
    )(ids, ext, own, other)


def local_terms(ids, ext, coef, cur, near, far, far_mid, far_top, pot, bond_cat, ang, prev, sent):
    step = 4

    def kernel(ids, ext, coef, cur, near, far, far_mid, far_top, pot, bond_cat, ang, *rest):
        prev, out = (rest[0], rest[1]) if len(rest) > 1 else (None, rest[0])
        first = pl.program_id(0) * step
        line = lax.broadcasted_iota(jnp.int32, (64, 256), 0)
        xs = [cur[:, r].reshape(64, 256) for r in range(step)]
        high, low = split(jnp.concatenate(xs, 0))
        angle = mm(high, ang[0]) + mm(low, ang[0]) + mm(high, ang[1])
        for r in range(step):
            part = slice(r * 64, r * 64 + 64)
            stack = jnp.concatenate([high[part], low[part], high[part]], 0)
            total = angle[part] + mm(bond_cat[...], stack)
            total = total + (pot[r] - SHIFT) * (1.0 / SPREAD) * xs[r]
            weight = coef[2 + first + r] * (1.0 / SPREAD)
            total = total - (weight * coef[0]) * near[:, r].reshape(64, 256)
            total = total - (weight * coef[1]) * jnp.concatenate(
                [f[:, r].reshape(-1, 256) for f in (far, far_mid, far_top)], 0
            )
            total = jnp.where(line < extent(ids, ext, first + r), total, 0.0)
            if prev is not None:
                total = 2.0 * total - prev[:, r].reshape(64, 256)
            out[:, r] = total.reshape(CHIPS, OCT, 256)

    whole = pl.BlockSpec((CHIPS, step, OCT, 256), lambda i: (0, i, 0, 0))
    def crossed(count):
        return pl.BlockSpec((count, step, OCT, 256), lambda i: (0, (i + 16 // step) % (32 // step), 0, 0))

    smem = pl.BlockSpec(memory_space=pltpu.SMEM)
    args = [ids, ext, coef, cur, near, far, far_mid, far_top, pot, bond_cat, ang]
    specs = [smem, smem, smem, whole, crossed(CHIPS), *[crossed(hi - lo) for lo, hi in BOUNDS], pl.BlockSpec((step, 64, 256), lambda i: (i, 0, 0))]
    specs += [
        pl.BlockSpec((64, 192), lambda i: (0, 0)),
        pl.BlockSpec((2, 256, 256), lambda i: (0, 0, 0)),
    ]
    if prev is not None:
        args.append(prev)
        specs.append(whole)
    return pl.pallas_call(
        kernel,
        grid=(32 // step,),
        in_specs=specs,
        out_specs=whole,
        out_shape=(pltpu.HBM if sent else jax.ShapeDtypeStruct)((CHIPS, 32, OCT, 256), F32),
        compiler_params=params(),
        cost_estimate=pl.CostEstimate(flops=2_000_000_000, bytes_accessed=14_000_000, transcendentals=0),
        name="local_terms",
    )(*args)


def radial_term(ids, ext_col, rad, packet, scale, more=None):
    rows = CHIPS * 32 * OCT
    flat = [p.reshape(rows, 256) for p in ((packet,) if more is None else (packet, more))]
    count = len(flat)

    def kernel(ids, ext_col, rad, *refs):
        ins, out = refs[:count], refs[count]

        def column(q):
            at = pl.ds(q, 256, stride=OCT)
            return ins[0][at, :] + ins[1][at, :] if count > 1 else ins[0][at, :]

        for q in range(0, OCT, 2):
            high, low = split(jnp.concatenate([column(q), column(q + 1)], 1))
            total = mm(rad[0], high) + mm(rad[0], low) + mm(rad[1], high)
            for i in range(2):
                half = total[:, i * 128 : i * 128 + 128]
                half = jnp.where(ext_col[...] > (ids[0] * OCT + q + i).astype(F32), half * scale, 0.0)
                out[pl.ds(q + i, 256, stride=OCT), :] = half

    lanes = pl.BlockSpec((rows, 128), lambda i: (0, i))
    full = pl.BlockSpec((2, 256, 256), lambda i: (0, 0, 0))
    out = pl.pallas_call(
        kernel,
        grid=(2,),
        in_specs=[
            pl.BlockSpec(memory_space=pltpu.SMEM), pl.BlockSpec((256, 128), lambda i: (0, 0)), full
        ] + [lanes] * count,
        out_specs=lanes,
        out_shape=pltpu.HBM((rows, 256), F32),
        compiler_params=params(56),
        cost_estimate=pl.CostEstimate(flops=2_000_000_000, bytes_accessed=5_000_000, transcendentals=0),
        name="radial_term",
    )(ids, ext_col, rad, *flat)
    return out.reshape(CHIPS, 32, OCT, 256)


def finish(ids, own, other, more=None):
    step = 2
    ins = (own, other) if more is None else (own, other, more)

    def kernel(ids, own, other, *rest):
        out = rest[-1]
        for o in range(step):
            at = slice(o * OCT, o * OCT + OCT)
            out[ids[1], :, at, :] = own[o] + rest[0][o] if len(rest) > 1 else own[o]
            out[1 - ids[1], :, at, :] = other[o]

    return pl.pallas_call(
        kernel,
        grid_spec=pltpu.PrefetchScalarGridSpec(
            num_scalar_prefetch=1,
            grid=(CHIPS // step,),
            in_specs=[pl.BlockSpec((step, 16, OCT, 256), lambda j, ids: (j, 0, 0, 0))] * len(ins),
            out_specs=pl.BlockSpec((2, 16, step * OCT, 256), lambda j, ids: (0, 0, j, 0)),
        ),
        out_shape=jax.ShapeDtypeStruct((2, 16, 64, 256), F32),
        compiler_params=params(),
        name="finish",
    )(ids, *ins)


def shards(initial_packet, extents, potential, coriolis_weight, radial_kinetic, bond_kinetic, angle_kinetic):
    ka, ga = lax.axis_index("ka"), lax.axis_index("ga")
    chip, core = ga // 2, ga % 2
    ids = jnp.stack([chip, core]).astype(jnp.int32)
    groups = lax.axis_size("ka")
    members = lax.axis_size("ga")
    top = jnp.float32((2 * groups - 1) * (2 * groups))

    def swap_core(x):
        return lax.ppermute(x, "ga", [(g, g ^ 1) for g in range(members)])

    def swap_far(x, count):
        pairs = [
            (i * members + g, k * members + (g ^ 1))
            for i in range(count)
            for g in range(members)
            for k in (i + 1 if g % 2 else i - 1,)
            if 0 <= k < count
        ]
        return lax.ppermute(x, ("ka", "ga"), pairs)

    def halo(t, turned):
        low, mid, top = [t[lo:hi] for lo, hi in BOUNDS]
        low, top = swap_far(low, groups), swap_far(top, groups // 2)
        turned, low, top = lax.optimization_barrier((turned, low, top))
        t, mid, turned = lax.optimization_barrier((t, mid, turned))
        return turned, (swap_core(t), low, swap_far(mid, groups), top)

    same_core = [list(range(c, members, 2)) for c in range(2)]

    def turn(x):
        return lax.all_to_all(x, "ga", 0, 0, axis_index_groups=same_core, tiled=True)

    other = swap_core(lax.dynamic_index_in_dim(initial_packet, 1 - core, 0, keepdims=False))
    pot = jnp.concatenate([potential, swap_core(potential)], 0)
    weight = jnp.concatenate([coriolis_weight, swap_core(coriolis_weight)])
    kvalue = (2 * ka + core).astype(F32)
    upper = jnp.sqrt(top - kvalue * (kvalue + 1.0))
    lower = jnp.where(kvalue > 0.0, jnp.sqrt(top - kvalue * (kvalue - 1.0)), 0.0)
    coef = jnp.concatenate(
        [jnp.stack([jnp.where(core == 0, upper, lower), jnp.where(core == 0, lower, upper)]), weight]
    )
    rad, bond_cat, ang, ext_col = prep(ids, radial_kinetic, bond_kinetic, angle_kinetic, extents)
    other, rad, bond_cat, ang, ext_col = lax.optimization_barrier((other, rad, bond_cat, ang, ext_col))

    def local(cur, halos, prev=None, sent=True):
        return local_terms(ids, extents, coef, cur, *halos, pot, bond_cat, ang, prev, sent)

    def radial(packet, scale, more=None):
        return radial_term(ids, ext_col, rad, packet, scale, more)

    t0 = start(ids, extents, initial_packet, other)
    turned, h0 = halo(t0, turn(t0))
    b0 = radial(turned, 1.0)
    a0 = local(t0, h0)
    t1 = a0 + turn(b0)
    turned, h1 = halo(t1, turn(a0))
    b1 = radial(turned, 2.0, b0)
    c1 = local(t1, h1, t0)
    t2 = c1 + turn(b1)
    turned, h2 = halo(t2, turn(c1))
    b2 = radial(turned, 2.0, b1)
    c2 = local(t2, h2, t1, sent=False)
    former = finish(ids, t2, swap_core(t2[:, 16:]))
    c2, former = lax.optimization_barrier((c2, former))
    b2 = turn(b2)
    newest = finish(ids, c2, swap_core(c2[:, 16:] + b2[:, 16:]), b2)
    return newest, former


def solution(mesh):
    return jax.shard_map(
        shards,
        mesh=mesh,
        in_specs=(
            P("ka", "ga", None, None),
            P("ka", None),
            P("ga", None, None),
            P("ga"),
            P(),
            P(),
            P(),
        ),
        out_specs=(P("ka", "ga", None, None), P("ka", "ga", None, None)),
        check_vma=False,
    )
```

```python
import functools

import jax
import jax.numpy as jnp
from jax import lax
from jax.experimental import pallas as pl
from jax.experimental.pallas import tpu as pltpu
from jax.sharding import PartitionSpec as P

SHIFT = 4.0
SPREAD = 7.0
CHIPS = 8
OCT = 8
BOUNDS = ((0, 3), (3, 5), (5, 8))
F32 = jnp.float32
BF16 = jnp.bfloat16


def split(x):
    high = x.astype(BF16)
    return high, (x - high.astype(F32)).astype(BF16)


def mm(a, b):
    return jnp.dot(a, b, preferred_element_type=F32)


def params(mib=24):
    return pltpu.CompilerParams(vmem_limit_bytes=mib * 1024 * 1024)


def extent(ids, ext, r):
    return ext[ids[1], ids[0] * 32 + ((r // 16) ^ ids[1]) * 16 + r % 16]


def prep(ids, radial, bond, angle, extents):
    def kernel(ids, radial, bond, angle, extents, rad, bond_cat, ang, ext_col, tmp, tmp_col):
        def rows(ref):
            return jnp.concatenate(
                [ref[pl.ds(pl.multiple_of((i ^ ids[1]) * 16, 16), 16), :] for i in range(16)], 0
            )

        tmp[...] = rows(radial).T
        rad[0], rad[1] = split(rows(tmp) / SPREAD)
        high, low = split(bond[...] / SPREAD)
        bond_cat[...] = jnp.concatenate([high, high, low], 1)
        ang[0], ang[1] = split(angle[...].T / SPREAD)
        line = jnp.where(ids[1] == 0, extents[0:1], extents[1:2]).astype(F32)
        tmp_col[...] = jnp.broadcast_to(line, (128, 256)).T
        ext_col[...] = rows(tmp_col)

    big = jax.ShapeDtypeStruct((2, 256, 256), BF16)
    vm = pl.BlockSpec(memory_space=pltpu.VMEM)
    return pl.pallas_call(
        kernel,
        out_shape=(big, jax.ShapeDtypeStruct((64, 192), BF16), big, jax.ShapeDtypeStruct((256, 128), F32)),
        in_specs=[pl.BlockSpec(memory_space=pltpu.SMEM), vm, vm, vm, vm],
        out_specs=(vm,) * 4,
        scratch_shapes=[pltpu.VMEM((256, 256), F32), pltpu.VMEM((256, 128), F32)],
        compiler_params=params(),
        name="prep",
    )(ids, radial, bond, angle, extents)


def start(ids, ext, own, other):
    step = 8
    half = 16 // step

    def kernel(ids, ext, own, other, whole):
        i = pl.program_id(0)
        line = lax.broadcasted_iota(jnp.int32, (64, 256), 0)
        for r in range(step):
            x = jnp.where(i < half, own[0, r], other[r])
            whole[:, r] = jnp.where(line < extent(ids, ext, i * step + r), x, 0.0).reshape(CHIPS, OCT, 256)

    return pl.pallas_call(
        kernel,
        grid_spec=pltpu.PrefetchScalarGridSpec(
            num_scalar_prefetch=2,
            grid=(32 // step,),
            in_specs=[
                pl.BlockSpec((1, step, 64, 256), lambda i, ids, ext: (ids[1], jnp.minimum(i, half - 1), 0, 0)),
                pl.BlockSpec((step, 64, 256), lambda i, ids, ext: (jnp.maximum(i - half, 0), 0, 0)),
            ],
            out_specs=pl.BlockSpec((CHIPS, step, OCT, 256), lambda i, ids, ext: (0, i, 0, 0)),
        ),
        out_shape=pltpu.HBM((CHIPS, 32, OCT, 256), F32),
        compiler_params=params(),
        name="start",
    )(ids, ext, own, other)


def local_terms(ids, ext, coef, cur, near, far, far_mid, far_top, pot, bond_cat, ang, prev, sent):
    step = 4

    def kernel(ids, ext, coef, cur, near, far, far_mid, far_top, pot, bond_cat, ang, *rest):
        prev, out = (rest[0], rest[1]) if len(rest) > 1 else (None, rest[0])
        first = pl.program_id(0) * step
        line = lax.broadcasted_iota(jnp.int32, (64, 256), 0)
        xs = [cur[:, r].reshape(64, 256) for r in range(step)]
        high, low = split(jnp.concatenate(xs, 0))
        angle = mm(
            jnp.concatenate([high, low, high], 1), jnp.concatenate([ang[0], ang[0], ang[1]], 0)
        )
        for r in range(step):
            part = slice(r * 64, r * 64 + 64)
            stack = jnp.concatenate([high[part], low[part], high[part]], 0)
            total = angle[part] + mm(bond_cat[...], stack)
            total = total + (pot[r] - SHIFT) * (1.0 / SPREAD) * xs[r]
            weight = coef[2 + first + r] * (1.0 / SPREAD)
            total = total - (weight * coef[0]) * near[:, r].reshape(64, 256)
            total = total - (weight * coef[1]) * jnp.concatenate(
                [f[:, r].reshape(-1, 256) for f in (far, far_mid, far_top)], 0
            )
            total = jnp.where(line < extent(ids, ext, first + r), total, 0.0)
            if prev is not None:
                total = 2.0 * total - prev[:, r].reshape(64, 256)
            out[:, r] = total.reshape(CHIPS, OCT, 256)

    whole = pl.BlockSpec((CHIPS, step, OCT, 256), lambda i: (0, i, 0, 0))
    def crossed(count):
        return pl.BlockSpec((count, step, OCT, 256), lambda i: (0, (i + 16 // step) % (32 // step), 0, 0))

    smem = pl.BlockSpec(memory_space=pltpu.SMEM)
    args = [ids, ext, coef, cur, near, far, far_mid, far_top, pot, bond_cat, ang]
    specs = [smem, smem, smem, whole, crossed(CHIPS), *[crossed(hi - lo) for lo, hi in BOUNDS], pl.BlockSpec((step, 64, 256), lambda i: (i, 0, 0))]
    specs += [
        pl.BlockSpec((64, 192), lambda i: (0, 0)),
        pl.BlockSpec((2, 256, 256), lambda i: (0, 0, 0)),
    ]
    if prev is not None:
        args.append(prev)
        specs.append(whole)
    return pl.pallas_call(
        kernel,
        grid=(32 // step,),
        in_specs=specs,
        out_specs=whole,
        out_shape=(pltpu.HBM if sent else jax.ShapeDtypeStruct)((CHIPS, 32, OCT, 256), F32),
        compiler_params=params(),
        cost_estimate=pl.CostEstimate(flops=2_000_000_000, bytes_accessed=14_000_000, transcendentals=0),
        name="local_terms",
    )(*args)


def radial_term(ids, ext_col, rad, packet, scale, more=None):
    rows = CHIPS * 32 * OCT
    flat = [p.reshape(rows, 256) for p in ((packet,) if more is None else (packet, more))]
    count = len(flat)

    def kernel(ids, ext_col, rad, *refs):
        ins, out = refs[:count], refs[count]

        def column(q):
            at = pl.ds(q, 256, stride=OCT)
            return ins[0][at, :] + ins[1][at, :] if count > 1 else ins[0][at, :]

        matrix = jnp.concatenate([rad[0], rad[0], rad[1]], 1)
        for q in range(0, OCT, 2):
            high, low = split(jnp.concatenate([column(q), column(q + 1)], 1))
            total = mm(matrix, jnp.concatenate([high, low, high], 0))
            for i in range(2):
                half = total[:, i * 128 : i * 128 + 128]
                half = jnp.where(ext_col[...] > (ids[0] * OCT + q + i).astype(F32), half * scale, 0.0)
                out[pl.ds(q + i, 256, stride=OCT), :] = half

    lanes = pl.BlockSpec((rows, 128), lambda i: (0, i))
    full = pl.BlockSpec((2, 256, 256), lambda i: (0, 0, 0))
    out = pl.pallas_call(
        kernel,
        grid=(2,),
        in_specs=[
            pl.BlockSpec(memory_space=pltpu.SMEM), pl.BlockSpec((256, 128), lambda i: (0, 0)), full
        ] + [lanes] * count,
        out_specs=lanes,
        out_shape=pltpu.HBM((rows, 256), F32),
        compiler_params=params(56),
        cost_estimate=pl.CostEstimate(flops=2_000_000_000, bytes_accessed=5_000_000, transcendentals=0),
        name="radial_term",
    )(ids, ext_col, rad, *flat)
    return out.reshape(CHIPS, 32, OCT, 256)


def finish(ids, own, other, more=None):
    step = 2
    ins = (own, other) if more is None else (own, other, more)

    def kernel(ids, own, other, *rest):
        out = rest[-1]
        for o in range(step):
            at = slice(o * OCT, o * OCT + OCT)
            out[ids[1], :, at, :] = own[o] + rest[0][o] if len(rest) > 1 else own[o]
            out[1 - ids[1], :, at, :] = other[o]

    return pl.pallas_call(
        kernel,
        grid_spec=pltpu.PrefetchScalarGridSpec(
            num_scalar_prefetch=1,
            grid=(CHIPS // step,),
            in_specs=[pl.BlockSpec((step, 16, OCT, 256), lambda j, ids: (j, 0, 0, 0))] * len(ins),
            out_specs=pl.BlockSpec((2, 16, step * OCT, 256), lambda j, ids: (0, 0, j, 0)),
        ),
        out_shape=jax.ShapeDtypeStruct((2, 16, 64, 256), F32),
        compiler_params=params(),
        name="finish",
    )(ids, *ins)


def shards(initial_packet, extents, potential, coriolis_weight, radial_kinetic, bond_kinetic, angle_kinetic):
    ka, ga = lax.axis_index("ka"), lax.axis_index("ga")
    chip, core = ga // 2, ga % 2
    ids = jnp.stack([chip, core]).astype(jnp.int32)
    groups = lax.axis_size("ka")
    members = lax.axis_size("ga")
    top = jnp.float32((2 * groups - 1) * (2 * groups))

    def swap_core(x):
        return lax.ppermute(x, "ga", [(g, g ^ 1) for g in range(members)])

    def swap_far(x, count):
        pairs = [
            (i * members + g, k * members + (g ^ 1))
            for i in range(count)
            for g in range(members)
            for k in (i + 1 if g % 2 else i - 1,)
            if 0 <= k < count
        ]
        return lax.ppermute(x, ("ka", "ga"), pairs)

    def halo(t, turned):
        low, mid, top = [t[lo:hi] for lo, hi in BOUNDS]
        low, top = swap_far(low, groups), swap_far(top, groups // 2)
        turned, low, top = lax.optimization_barrier((turned, low, top))
        t, mid, turned = lax.optimization_barrier((t, mid, turned))
        return turned, (swap_core(t), low, swap_far(mid, groups), top)

    same_core = [list(range(c, members, 2)) for c in range(2)]

    def turn(x):
        return lax.all_to_all(x, "ga", 0, 0, axis_index_groups=same_core, tiled=True)

    other = swap_core(lax.dynamic_index_in_dim(initial_packet, 1 - core, 0, keepdims=False))
    pot = jnp.concatenate([potential, swap_core(potential)], 0)
    weight = jnp.concatenate([coriolis_weight, swap_core(coriolis_weight)])
    kvalue = (2 * ka + core).astype(F32)
    upper = jnp.sqrt(top - kvalue * (kvalue + 1.0))
    lower = jnp.where(kvalue > 0.0, jnp.sqrt(top - kvalue * (kvalue - 1.0)), 0.0)
    coef = jnp.concatenate(
        [jnp.stack([jnp.where(core == 0, upper, lower), jnp.where(core == 0, lower, upper)]), weight]
    )
    rad, bond_cat, ang, ext_col = prep(ids, radial_kinetic, bond_kinetic, angle_kinetic, extents)
    other, rad, bond_cat, ang, ext_col = lax.optimization_barrier((other, rad, bond_cat, ang, ext_col))

    def local(cur, halos, prev=None, sent=True):
        return local_terms(ids, extents, coef, cur, *halos, pot, bond_cat, ang, prev, sent)

    def radial(packet, scale, more=None):
        return radial_term(ids, ext_col, rad, packet, scale, more)

    t0 = start(ids, extents, initial_packet, other)
    turned, h0 = halo(t0, turn(t0))
    b0 = radial(turned, 1.0)
    a0 = local(t0, h0)
    t1 = a0 + turn(b0)
    turned, h1 = halo(t1, turn(a0))
    b1 = radial(turned, 2.0, b0)
    c1 = local(t1, h1, t0)
    t2 = c1 + turn(b1)
    turned, h2 = halo(t2, turn(c1))
    b2 = radial(turned, 2.0, b1)
    c2 = local(t2, h2, t1, sent=False)
    former = finish(ids, t2, swap_core(t2[:, 16:]))
    c2, former = lax.optimization_barrier((c2, former))
    b2 = turn(b2)
    newest = finish(ids, c2, swap_core(c2[:, 16:] + b2[:, 16:]), b2)
    return newest, former


def solution(mesh):
    return jax.shard_map(
        shards,
        mesh=mesh,
        in_specs=(
            P("ka", "ga", None, None),
            P("ka", None),
            P("ga", None, None),
            P("ga"),
            P(),
            P(),
            P(),
        ),
        out_specs=(P("ka", "ga", None, None), P("ka", "ga", None, None)),
        check_vma=False,
    )
```
